32 devices in a mesh: client: 8 (over z, core), param: 4 (over y, x).
Axes of the slice: x: 2, y: 2, z: 4, core: 2. Of those that a mesh axis runs over, the one named last changes fastest.
Arguments:
- inputs: bfloat16 [8, 384, 2304], P('client', None, 'param'), may hold values from -6 to 6
- targets: bfloat16 [8, 384, 2304], P('client', None, 'param'), may hold values from -35 to 35
- norm_gain: float32 [2304], replicated, may hold values from 0.1 to 1.9
- gate_weight: bfloat16 [2304, 4608], P(None, 'param'), may hold values from -0.125 to 0.125
- up_weight: bfloat16 [2304, 4608], P(None, 'param'), may hold values from -0.125 to 0.125
- down_weight: bfloat16 [4608, 2304], P('param'), may hold values from -0.09375 to 0.09375
- neighbours: int32 [8], replicated, may hold values from 3 to 6
Outputs:
- update_gate: float32 [2304, 4608], P('client', 'param')
- update_up: float32 [2304, 4608], P('client', 'param')
- update_down: float32 [2304, 4608], P('client', 'param')
- relative_weight: float32 [8], replicated
The draws below stay inside these ranges and needn't reach their ends.
All inputs are finite; a program needn't handle non-finite values.
Results may differ from the reference program's by a relative error of at most 0.0095.
Values may be sent and summed in bfloat16 or wider, within the bound.
A program may use at most 128 MiB of HBM per device.

```python
import math
import jax
import jax.numpy as jnp
from jax import lax

D = 2304
FFW = 4608
TOK = 384
CLIENTS = 8
N_CLIENT = 8
N_PARAM = 4


def draw_targets(key, part):
    key_parts = jax.random.split(key, 3)
    client_scale = jnp.exp(jax.random.uniform(key_parts[0], (CLIENTS, 1, 1), jnp.float32, -1.0, 1.0))
    column_scale = jnp.exp(jax.random.uniform(key_parts[1], (1, 1, D), jnp.float32, -1.15, 1.15))
    base_draw = jnp.clip(jax.random.normal(key_parts[2], (CLIENTS, TOK, D), jnp.float32), -4.0, 4.0)
    return (base_draw * client_scale * column_scale).astype(jnp.bfloat16)


def touch_ends(values, key, smallest, high):
    shape = values.shape
    place = [jax.random.randint(jax.random.fold_in(key, axis), (), 0, shape[axis]) for axis in range(len(shape))]
    values = values.at[tuple(place)].set(smallest)
    longest = shape.index(max(shape))
    place[longest] = (place[longest] + 1) % shape[longest]
    return values.at[tuple(place)].set(high)


def steps_of(rng, dims, cuts, low, top_value):
    level = 1.0
    for axis_at, parts in cuts:
        steps = jax.random.uniform(jax.random.fold_in(jax.random.fold_in(rng, 6), axis_at), (parts,), jnp.float32, low / len(cuts), top_value / len(cuts))
        level = level * jnp.repeat(jnp.exp(steps), dims[axis_at] // parts).reshape((-1,) + (1,) * (len(dims) - 1 - axis_at))
    return level


def normal_values(stream_key, extent, scale, most, shards=(), held_as=jnp.bfloat16):
    entries = scale * jax.random.normal(stream_key, extent, jnp.float32)
    if shards:
        entries = entries * steps_of(stream_key, extent, shards, -0.22, 0.18)
    return jnp.clip(entries, -most, most).astype(held_as)


def setup_inputs(seed: int = 0) -> dict:
    streams_of = jax.random.split(jax.random.key(seed), 8)
    return {
        "inputs": normal_values(streams_of[0], (CLIENTS, TOK, D), 1.0, 6.0, ((0, 8), (2, 4))),
        "targets": draw_targets(jax.random.fold_in(streams_of[7], 71), 0),
        "norm_gain": jnp.clip(1.0 + 0.18 * jax.random.normal(streams_of[2], (D,), jnp.float32), 0.1, 1.9),
        "gate_weight": normal_values(streams_of[3], (D, FFW), D ** -0.5, 0.125, ((1, 4),)),
        "up_weight": normal_values(streams_of[4], (D, FFW), D ** -0.5, 0.125, ((1, 4),)),
        "down_weight": normal_values(streams_of[5], (FFW, D), FFW ** -0.5, 0.09375, ((0, 4),)),
        "neighbours": touch_ends(jax.random.randint(streams_of[6], (CLIENTS,), N_CLIENT // 4 + 1, N_CLIENT - 1), jax.random.fold_in(streams_of[6], 1), N_CLIENT // 4 + 1, (N_CLIENT - 1) - 1).astype(jnp.int32),
    }


def gelu_tanh(values):
    return jax.nn.gelu(values, approximate=True)

def rms_normed(gathered, norm_gain):
    widened = gathered.astype(jnp.float32)
    inverse_rms = lax.rsqrt(lax.optimization_barrier(jnp.mean(widened * widened, axis=-1, keepdims=True)) + 1e-06)
    return (widened * inverse_rms * norm_gain.astype(jnp.float32)).astype(jnp.bfloat16)

def krum_weights(gram, neighbours):
    client_count = gram.shape[0]
    diagonal = jnp.diagonal(gram)
    distance = diagonal[:, None] + diagonal[None, :] - 2.0 * gram
    row_index = lax.broadcasted_iota(jnp.int32, (client_count, client_count), 0)
    col_index = lax.broadcasted_iota(jnp.int32, (client_count, client_count), 1)
    distance = jnp.where(row_index == col_index, jnp.asarray(1e+30, gram.dtype), distance)
    ordered = jnp.sort(distance, axis=1)
    scores = lax.optimization_barrier(jnp.sum(jnp.where(col_index < neighbours[:, None], ordered, jnp.zeros_like(ordered)), axis=1))
    scaled = scores / jnp.mean(scores)
    exponent = jnp.exp(-4.0 * scaled)
    return exponent / jnp.sum(exponent)

def reference(inputs, targets, norm_gain, gate_weight, up_weight, down_weight, neighbours):
    factor = 1.0 / math.sqrt(TOK)
    highest = lax.Precision.HIGHEST

    def client_pass(pair_rows):
        client_rows, target_rows = pair_rows
        normed = rms_normed(client_rows, norm_gain)
        gate_value = jnp.dot(normed, gate_weight, preferred_element_type=jnp.float32)
        up_value = jnp.dot(normed, up_weight, preferred_element_type=jnp.float32)
        activated, gelu_back = jax.vjp(gelu_tanh, gate_value)
        hidden = (activated * up_value).astype(jnp.bfloat16)
        out_value = jnp.dot(hidden, down_weight, preferred_element_type=jnp.float32)
        residual = ((out_value - target_rows.astype(jnp.float32)) * factor).astype(jnp.bfloat16)
        back_hidden = lax.dot_general(residual, down_weight, (((1,), (1,)), ((), ())), preferred_element_type=jnp.float32)
        grad_act = gelu_back(back_hidden * up_value)[0]
        back_gate = grad_act.astype(jnp.bfloat16)
        back_up = (back_hidden * activated).astype(jnp.bfloat16)
        return (normed, residual, hidden, back_gate, back_up)
    normed, residual, hidden, back_gate, back_up = lax.map(client_pass, (inputs, targets))
    normed_wide = normed.astype(jnp.float32)
    residual_wide = residual.astype(jnp.float32)
    block_size = FFW // N_PARAM
    offsets = jnp.arange(N_PARAM, dtype=jnp.int32) * block_size

    def deltas_at(offset):

        def columns(array):
            return lax.dynamic_slice_in_dim(array, offset, block_size, 2).astype(jnp.float32)
        gate_delta = (-jnp.einsum('ctd,ctf->cdf', normed_wide, columns(back_gate), precision=highest)).astype(jnp.bfloat16)
        up_delta = (-jnp.einsum('ctd,ctf->cdf', normed_wide, columns(back_up), precision=highest)).astype(jnp.bfloat16)
        down_delta = (-jnp.einsum('ctd,ctf->cdf', residual_wide, columns(hidden), precision=highest)).astype(jnp.bfloat16)
        return (gate_delta, up_delta, down_delta)

    def gram_step(running, offset):
        for delta_block in deltas_at(offset):
            widened = delta_block.astype(jnp.float32)
            running = running + jnp.einsum('cdf,edf->ce', widened, widened, precision=highest)
        return (running, None)
    gram, _ = lax.scan(gram_step, jnp.zeros((N_CLIENT, N_CLIENT), jnp.float32), offsets)
    weights = krum_weights(gram, neighbours)

    def update_step(offset):
        return tuple((lax.optimization_barrier(jnp.sum(weights[:, None, None] * delta_block.astype(jnp.float32), axis=0)) for delta_block in deltas_at(offset)))
    blocks = lax.map(update_step, offsets)

    def assemble(stacked):
        return jnp.transpose(stacked, (1, 0, 2)).reshape(D, FFW)
    return (assemble(blocks[0]), assemble(blocks[1]), assemble(blocks[2]), N_CLIENT * weights)
```

```python
import functools
import math

import jax
import jax.numpy as jnp
from jax import lax
from jax.experimental import pallas as pl
from jax.experimental.pallas import tpu as pltpu
from jax.sharding import PartitionSpec as P


def gelu_tanh(values):
    return jax.nn.gelu(values, approximate=True)


def rms_normed(gathered, norm_gain):
    widened = gathered.astype(jnp.float32)
    inverse_rms = lax.rsqrt(jnp.mean(widened * widened, axis=-1, keepdims=True) + 1e-06)
    return (widened * inverse_rms * norm_gain).astype(jnp.bfloat16)


def krum_weights(gram, neighbours):
    client_count = gram.shape[0]
    diagonal = jnp.diagonal(gram)
    distance = diagonal[:, None] + diagonal[None, :] - 2.0 * gram
    row_index = lax.broadcasted_iota(jnp.int32, (client_count, client_count), 0)
    col_index = lax.broadcasted_iota(jnp.int32, (client_count, client_count), 1)
    distance = jnp.where(row_index == col_index, jnp.asarray(1e30, gram.dtype), distance)
    ordered = jnp.sort(distance, axis=1)
    scores = jnp.sum(
        jnp.where(col_index < neighbours[:, None], ordered, jnp.zeros_like(ordered)), axis=1
    )
    scaled = scores / jnp.mean(scores)
    exponent = jnp.exp(-4.0 * scaled)
    return exponent / jnp.sum(exponent)


def token_contract(left, right):
    return lax.dot_general(
        left, right, (((0,), (0,)), ((), ())), preferred_element_type=jnp.float32
    )


def pair_products(exchanged):
    flattened = exchanged.reshape(exchanged.shape[0], -1)
    return lax.dot_general(
        flattened, flattened, (((1,), (1,)), ((), ())), preferred_element_type=jnp.float32
    )


def weighted_sum(weights, exchanged):
    return jnp.sum(weights[:, None, None] * exchanged.astype(jnp.float32), axis=0)


def on_device(inputs, targets, norm_gain, gate_weight, up_weight, down_weight, neighbours):
    token_count = inputs.shape[1]
    factor = 1.0 / math.sqrt(token_count)
    gathered = lax.all_gather(inputs, "param", axis=2, tiled=True)
    normed = rms_normed(gathered[0], norm_gain)
    gate_value = jnp.dot(normed, gate_weight, preferred_element_type=jnp.float32)
    up_value = jnp.dot(normed, up_weight, preferred_element_type=jnp.float32)
    activated, gelu_back = jax.vjp(gelu_tanh, gate_value)
    hidden = (activated * up_value).astype(jnp.bfloat16)
    partial_out = jnp.dot(hidden, down_weight, preferred_element_type=jnp.float32)
    out_share = lax.psum_scatter(
        partial_out.astype(jnp.bfloat16), "param", scatter_dimension=1, tiled=True
    ).astype(jnp.float32)
    local_residual = ((out_share - targets[0].astype(jnp.float32)) * factor).astype(jnp.bfloat16)
    residual = lax.all_gather(local_residual, "param", axis=1, tiled=True)
    down_delta = (-token_contract(residual, hidden)).astype(jnp.bfloat16)
    back_hidden = lax.dot_general(
        residual, down_weight, (((1,), (1,)), ((), ())), preferred_element_type=jnp.float32
    )
    back_gate = gelu_back(back_hidden * up_value)[0].astype(jnp.bfloat16)
    back_up = (back_hidden * activated).astype(jnp.bfloat16)
    gate_delta = (-token_contract(normed, back_gate)).astype(jnp.bfloat16)
    up_delta = (-token_contract(normed, back_up)).astype(jnp.bfloat16)
    owned_gate, owned_up, owned_down = (
        lax.all_to_all(gate_delta[None], "client", split_axis=1, concat_axis=0, tiled=True),
        lax.all_to_all(up_delta[None], "client", split_axis=1, concat_axis=0, tiled=True),
        lax.all_to_all(down_delta[None], "client", split_axis=1, concat_axis=0, tiled=True),
    )
    partial_gram = pair_products(owned_gate) + pair_products(owned_up) + pair_products(owned_down)
    gram = lax.psum(partial_gram, ("client", "param"))
    weights = krum_weights(gram, neighbours)
    client_count = lax.axis_size("client")
    update_gate = weighted_sum(weights, owned_gate)
    update_up = weighted_sum(weights, owned_up)
    update_down = weighted_sum(weights, owned_down)
    return (update_gate, update_up, update_down, client_count * weights)

PAIR = 2


def delta_gram_kernel(left_ref, right_ref, delta_ref, gram_ref, totals):
    clients, rows, columns = delta_ref.shape

    @pl.when((pl.program_id(0) == 0) & (pl.program_id(1) == 0))
    def _():
        totals[...] = jnp.zeros_like(totals)

    for client in range(clients):
        product = jnp.dot(left_ref[client], right_ref[client], preferred_element_type=jnp.float32)
        delta_ref[client] = (-product).astype(jnp.bfloat16)

    pairs = [(i, j) for i in range(clients) for j in range(i, clients)]
    lanes = columns // 128 * 128
    tail = columns - lanes

    def accumulate(row, at, width, sums):
        tiles = [
            delta_ref[client, pl.ds(row, 16), at : at + width].astype(jnp.float32)
            for client in range(clients)
        ]
        found = []
        for (i, j), total in zip(pairs, sums):
            product = tiles[i] * tiles[j]
            found.append(total + (product[:8] + product[8:]))
        return tuple(found)

    def step(index, sums):
        row = pl.multiple_of(index * 16, 16)
        for at in range(0, lanes, 128):
            sums = accumulate(row, at, 128, sums)
        return sums

    zeros = tuple(jnp.zeros((8, 128), jnp.float32) for _ in pairs)
    sums = lax.fori_loop(0, rows // 16, step, zeros)
    for at, total in enumerate(sums):
        totals[at] += total
    if tail:

        def tail_step(index, sums):
            return accumulate(pl.multiple_of(index * 16, 16), lanes, tail, sums)

        zeros = tuple(jnp.zeros((8, tail), jnp.float32) for _ in pairs)
        sums = lax.fori_loop(0, rows // 16, tail_step, zeros)
        for at, total in enumerate(sums):
            totals[at, :, :tail] += total

    last = (pl.program_id(0) == pl.num_programs(0) - 1) & (
        pl.program_id(1) == pl.num_programs(1) - 1
    )

    @pl.when(last)
    def _():
        gram_ref[...] = jnp.sum(totals[...], axis=1)


def deltas_and_gram(left, right):
    _, clients, rows, tokens = left.shape
    columns = right.shape[3]
    row_tile = 96 if rows % 96 == 0 else rows
    pair_count = clients * (clients + 1) // 2
    deltas, sums = pl.pallas_call(
        delta_gram_kernel,
        grid=(3, rows // row_tile),
        in_specs=[
            pl.BlockSpec((None, clients, row_tile, tokens), lambda kind, at: (kind // 2, 0, at, 0)),
            pl.BlockSpec((None, clients, tokens, columns), lambda kind, at: (kind, 0, 0, 0)),
        ],
        out_specs=[
            pl.BlockSpec((None, clients, row_tile, columns), lambda kind, at: (kind, 0, at, 0)),
            pl.BlockSpec((pair_count, 128), lambda kind, at: (0, 0)),
        ],
        out_shape=[
            jax.ShapeDtypeStruct((3, clients, rows, columns), jnp.bfloat16),
            jax.ShapeDtypeStruct((pair_count, 128), jnp.float32),
        ],
        scratch_shapes=[pltpu.VMEM((pair_count, 8, 128), jnp.float32)],
        compiler_params=pltpu.CompilerParams(vmem_limit_bytes=48 * 2**20),
        cost_estimate=pl.CostEstimate(
            flops=6 * clients * rows * tokens * columns, bytes_accessed=40 * 2**20, transcendentals=0
        ),
        name="deltas_and_gram",
    )(left, right)
    upper = jnp.sum(sums, axis=1)
    index = jnp.asarray([[place_count(clients, min(i, j), max(i, j)) for j in range(clients)] for i in range(clients)])
    return deltas, upper[index]


def place_count(clients, i, j):
    return i * clients - i * (i - 1) // 2 + (j - i)


def laid_out(gathered):
    clients, params, tokens, width = gathered.shape
    return gathered.transpose(0, 2, 1, 3).reshape(clients, tokens, params * width)


def on_device_shared(inputs, targets, norm_gain, gate_weight, up_weight, down_weight, neighbours):
    token_count = inputs.shape[1]
    clients = lax.axis_size("client")
    params = lax.axis_size("param")
    client = lax.axis_index("client")
    width = inputs.shape[2]
    depth = width * params
    core = client % PAIR
    half = gate_weight.shape[1] // PAIR
    chip_rows = depth // clients * PAIR
    factor = 1.0 / math.sqrt(token_count)

    own = lax.all_gather(inputs, "param", axis=2, tiled=True)[0]
    every_input = lax.all_gather(inputs[0], ("client", "param"), axis=0)
    normed_own = rms_normed(own, norm_gain)
    gate_value = jnp.dot(normed_own, gate_weight, preferred_element_type=jnp.float32)
    up_value = jnp.dot(normed_own, up_weight, preferred_element_type=jnp.float32)
    hidden = (gelu_tanh(gate_value) * up_value).astype(jnp.bfloat16)
    partial_out = jnp.dot(hidden, down_weight, preferred_element_type=jnp.float32)
    out_share = lax.psum_scatter(
        partial_out.astype(jnp.bfloat16), "param", scatter_dimension=1, tiled=True
    ).astype(jnp.float32)
    local_residual = ((out_share - targets[0].astype(jnp.float32)) * factor).astype(jnp.bfloat16)
    every_residual = lax.all_gather(local_residual, ("client", "param"), axis=0)

    gate_half = lax.dynamic_slice_in_dim(gate_weight, core * half, half, 1)
    up_half = lax.dynamic_slice_in_dim(up_weight, core * half, half, 1)
    down_half = lax.dynamic_slice_in_dim(down_weight, core * half, half, 0)
    shape = (clients, params, token_count, width)
    normed = rms_normed(laid_out(every_input.reshape(shape)), norm_gain)
    residual = laid_out(every_residual.reshape(shape))
    gate_value = jnp.dot(normed, gate_half, preferred_element_type=jnp.float32)
    up_value = jnp.dot(normed, up_half, preferred_element_type=jnp.float32)
    activated, gelu_back = jax.vjp(gelu_tanh, gate_value)
    hidden = (activated * up_value).astype(jnp.bfloat16)
    back_hidden = lax.dot_general(
        residual, down_half, (((2,), (1,)), ((), ())), preferred_element_type=jnp.float32
    )
    back_gate = gelu_back(back_hidden * up_value)[0].astype(jnp.bfloat16)
    back_up = (back_hidden * activated).astype(jnp.bfloat16)
    rows_at = client // PAIR * chip_rows
    left = jnp.stack(
        [
            lax.dynamic_slice_in_dim(array, rows_at, chip_rows, 2).transpose(0, 2, 1)
            for array in (normed, residual)
        ]
    )
    deltas, partial_gram = deltas_and_gram(left, jnp.stack([back_gate, back_up, hidden]))
    gram = lax.psum(partial_gram, ("client", "param"))
    weights = krum_weights(gram, neighbours)
    updates = jnp.sum(weights[None, :, None, None] * deltas.astype(jnp.float32), axis=1)
    updates = updates.reshape(3, PAIR, chip_rows // PAIR, half)
    kept = lax.dynamic_index_in_dim(updates, core, 1, keepdims=False)
    sent = lax.dynamic_index_in_dim(updates, 1 - core, 1, keepdims=False)
    arrived = lax.ppermute(sent, "client", [(i, i ^ 1) for i in range(clients)])
    first = jnp.where(core == 0, kept, arrived)
    second = jnp.where(core == 0, arrived, kept)
    whole = jnp.concatenate([first, second], axis=2)
    return (whole[0], whole[1], whole[2], clients * weights)


def solution(mesh):
    in_specs = (
        P("client", None, "param"),
        P("client", None, "param"),
        P(),
        P(None, "param"),
        P(None, "param"),
        P("param", None),
        P(),
    )
    out_specs = (P("client", "param"), P("client", "param"), P("client", "param"), P())
    shared = mesh.shape["client"] <= 8 and mesh.shape["client"] % PAIR == 0
    body = on_device_shared if shared else on_device
    return jax.shard_map(
        body, mesh=mesh, in_specs=in_specs, out_specs=out_specs, check_vma=False
    )
```

```python
import functools
import math

import jax
import jax.numpy as jnp
from jax import lax
from jax.experimental import pallas as pl
from jax.experimental.pallas import tpu as pltpu
from jax.sharding import PartitionSpec as P


def gelu_tanh(values):
    return jax.nn.gelu(values, approximate=True)


def rms_normed(gathered, norm_gain):
    widened = gathered.astype(jnp.float32)
    inverse_rms = lax.rsqrt(jnp.mean(widened * widened, axis=-1, keepdims=True) + 1e-06)
    return (widened * inverse_rms * norm_gain).astype(jnp.bfloat16)


def krum_weights(gram, neighbours):
    client_count = gram.shape[0]
    diagonal = jnp.diagonal(gram)
    distance = diagonal[:, None] + diagonal[None, :] - 2.0 * gram
    row_index = lax.broadcasted_iota(jnp.int32, (client_count, client_count), 0)
    col_index = lax.broadcasted_iota(jnp.int32, (client_count, client_count), 1)
    distance = jnp.where(row_index == col_index, jnp.asarray(1e30, gram.dtype), distance)
    ordered = jnp.sort(distance, axis=1)
    scores = jnp.sum(
        jnp.where(col_index < neighbours[:, None], ordered, jnp.zeros_like(ordered)), axis=1
    )
    scaled = scores / jnp.mean(scores)
    exponent = jnp.exp(-4.0 * scaled)
    return exponent / jnp.sum(exponent)


def token_contract(left, right):
    return lax.dot_general(
        left, right, (((0,), (0,)), ((), ())), preferred_element_type=jnp.float32
    )


def pair_products(exchanged):
    flattened = exchanged.reshape(exchanged.shape[0], -1)
    return lax.dot_general(
        flattened, flattened, (((1,), (1,)), ((), ())), preferred_element_type=jnp.float32
    )


def weighted_sum(weights, exchanged):
    return jnp.sum(weights[:, None, None] * exchanged.astype(jnp.float32), axis=0)


def on_device(inputs, targets, norm_gain, gate_weight, up_weight, down_weight, neighbours):
    token_count = inputs.shape[1]
    factor = 1.0 / math.sqrt(token_count)
    gathered = lax.all_gather(inputs, "param", axis=2, tiled=True)
    normed = rms_normed(gathered[0], norm_gain)
    gate_value = jnp.dot(normed, gate_weight, preferred_element_type=jnp.float32)
    up_value = jnp.dot(normed, up_weight, preferred_element_type=jnp.float32)
    activated, gelu_back = jax.vjp(gelu_tanh, gate_value)
    hidden = (activated * up_value).astype(jnp.bfloat16)
    partial_out = jnp.dot(hidden, down_weight, preferred_element_type=jnp.float32)
    out_share = lax.psum_scatter(
        partial_out.astype(jnp.bfloat16), "param", scatter_dimension=1, tiled=True
    ).astype(jnp.float32)
    local_residual = ((out_share - targets[0].astype(jnp.float32)) * factor).astype(jnp.bfloat16)
    residual = lax.all_gather(local_residual, "param", axis=1, tiled=True)
    down_delta = (-token_contract(residual, hidden)).astype(jnp.bfloat16)
    back_hidden = lax.dot_general(
        residual, down_weight, (((1,), (1,)), ((), ())), preferred_element_type=jnp.float32
    )
    back_gate = gelu_back(back_hidden * up_value)[0].astype(jnp.bfloat16)
    back_up = (back_hidden * activated).astype(jnp.bfloat16)
    gate_delta = (-token_contract(normed, back_gate)).astype(jnp.bfloat16)
    up_delta = (-token_contract(normed, back_up)).astype(jnp.bfloat16)
    owned_gate, owned_up, owned_down = (
        lax.all_to_all(gate_delta[None], "client", split_axis=1, concat_axis=0, tiled=True),
        lax.all_to_all(up_delta[None], "client", split_axis=1, concat_axis=0, tiled=True),
        lax.all_to_all(down_delta[None], "client", split_axis=1, concat_axis=0, tiled=True),
    )
    partial_gram = pair_products(owned_gate) + pair_products(owned_up) + pair_products(owned_down)
    gram = lax.psum(partial_gram, ("client", "param"))
    weights = krum_weights(gram, neighbours)
    client_count = lax.axis_size("client")
    update_gate = weighted_sum(weights, owned_gate)
    update_up = weighted_sum(weights, owned_up)
    update_down = weighted_sum(weights, owned_down)
    return (update_gate, update_up, update_down, client_count * weights)

PAIR = 2


def gelu_parts(values):
    scale = math.sqrt(2.0 / math.pi)
    squared = values * values
    bent = jnp.tanh(scale * values * (1.0 + 0.044715 * squared))
    lifted = 0.5 * (1.0 + bent)
    slope = 0.5 * values * (1.0 - bent * bent) * scale * (1.0 + 3.0 * 0.044715 * squared)
    return values * lifted, lifted + slope


def forward_kernel(
    rows_ref, gain_ref, gate_ref, up_ref, slope_ref, active_ref, hidden_ref, block_ref, normed
):
    params, _, width = rows_ref.shape
    chip = lax.axis_index("client") // PAIR
    total = 0.0
    for at in range(params):
        wide = rows_ref[at].astype(jnp.float32)
        total += jnp.sum(wide * wide, axis=1, keepdims=True)
    inverse = lax.rsqrt(total * (1.0 / (params * width)) + 1e-06)
    for at in range(params):
        wide = rows_ref[at].astype(jnp.float32)
        normed[:, at * width : (at + 1) * width] = (wide * inverse * gain_ref[at]).astype(jnp.bfloat16)
    block_ref[...] = (rows_ref[chip].astype(jnp.float32) * inverse * gain_ref[chip]).astype(jnp.bfloat16)
    gate = jnp.dot(normed[...], gate_ref[...], preferred_element_type=jnp.float32)
    up = jnp.dot(normed[...], up_ref[...], preferred_element_type=jnp.float32)
    active, slope = gelu_parts(gate)
    slope_ref[...] = slope * up
    active_ref[...] = active
    hidden_ref[...] = (active * up).astype(jnp.bfloat16)


def forward_all(every_input, norm_gain, gate_half, up_half):
    clients, params, tokens, width = every_input.shape
    depth, half = gate_half.shape
    client_block = lambda shape: pl.BlockSpec((None,) + shape, lambda at: (at,) + (0,) * len(shape))
    whole = lambda shape: pl.BlockSpec(shape, lambda at: (0,) * len(shape))
    return pl.pallas_call(
        forward_kernel,
        grid=(clients,),
        in_specs=[
            client_block((params, tokens, width)),
            whole((params, 1, width)),
            whole((depth, half)),
            whole((depth, half)),
        ],
        out_specs=[client_block((tokens, half))] * 3 + [client_block((tokens, width))],
        out_shape=[
            jax.ShapeDtypeStruct((clients, tokens, half), jnp.float32),
            jax.ShapeDtypeStruct((clients, tokens, half), jnp.float32),
            jax.ShapeDtypeStruct((clients, tokens, half), jnp.bfloat16),
            jax.ShapeDtypeStruct((clients, tokens, width), jnp.bfloat16),
        ],
        scratch_shapes=[pltpu.VMEM((tokens, depth), jnp.bfloat16)],
        compiler_params=pltpu.CompilerParams(vmem_limit_bytes=56 * 2**20),
        cost_estimate=pl.CostEstimate(
            flops=4 * clients * tokens * depth * half, bytes_accessed=40 * 2**20, transcendentals=0
        ),
        name="forward_all",
    )(every_input, norm_gain.reshape(params, 1, width), gate_half, up_half)


def backward_kernel(
    rows_ref, slope_ref, active_ref, hidden_ref, block_ref, down_ref, delta_ref, gram_ref,
    residual, held, totals,
):
    params, _, width = rows_ref.shape
    _, clients, rows, columns = held.shape
    step_at = pl.program_id(0)
    chip = lax.axis_index("client") // PAIR
    for at in range(params):
        residual[:, at * width : (at + 1) * width] = rows_ref[at]
    back = lax.dot_general(
        residual[...], down_ref[...], (((1,), (1,)), ((), ())), preferred_element_type=jnp.float32
    )
    back_gate = (back * slope_ref[...]).astype(jnp.bfloat16)
    back_up = (back * active_ref[...]).astype(jnp.bfloat16)
    for kind, (left, right) in enumerate(
        ((block_ref[...], back_gate), (block_ref[...], back_up), (rows_ref[chip], hidden_ref[...]))
    ):
        delta = (-token_contract(left, right)).astype(jnp.bfloat16)
        delta_ref[kind] = delta
        held[kind, step_at] = delta

    @pl.when(step_at == clients - 1)
    def _():
        totals[...] = jnp.zeros_like(totals)
        pairs = [(i, j) for i in range(clients) for j in range(i, clients)]
        starts = [(at, min(128, columns - at)) for at in range(0, columns, 128)]

        def add_up(kind, begin, wide, repeat):
            def step(index, sums):
                row = pl.multiple_of(index * 16, 16)
                for at in range(begin, begin + wide * repeat, wide):
                    tiles = [
                        held[kind, client, pl.ds(row, 16), at : at + wide].astype(jnp.float32)
                        for client in range(clients)
                    ]
                    found = []
                    for (i, j), total in zip(pairs, sums):
                        product = tiles[i] * tiles[j]
                        found.append(total + (product[:8] + product[8:]))
                    sums = tuple(found)
                return sums

            zeros = tuple(jnp.zeros((8, wide), jnp.float32) for _ in pairs)
            sums = lax.fori_loop(0, rows // 16, step, zeros)
            for at, total in enumerate(sums):
                totals[at, :, :wide] += total

        lanes = columns // 128 * 128
        for kind in range(3):
            add_up(kind, 0, 128, lanes // 128)
            if columns - lanes:
                add_up(kind, lanes, columns - lanes, 1)
        gram_ref[...] = jnp.zeros_like(gram_ref)
        gram_ref[: len(pairs), :] = jnp.sum(totals[...], axis=1)


def backward_all(every_residual, slope, active, hidden, block, down_half):
    clients, params, tokens, width = every_residual.shape
    half, depth = down_half.shape
    pair_count = clients * (clients + 1) // 2
    padded = -(-pair_count // 8) * 8
    client_block = lambda shape: pl.BlockSpec((None,) + shape, lambda at: (at,) + (0,) * len(shape))
    return pl.pallas_call(
        backward_kernel,
        grid=(clients,),
        in_specs=[client_block((params, tokens, width))]
        + [client_block((tokens, half))] * 3
        + [client_block((tokens, width)), pl.BlockSpec((half, depth), lambda at: (0, 0))],
        out_specs=[
            pl.BlockSpec((3, None, width, half), lambda at: (0, at, 0, 0)),
            pl.BlockSpec((padded, 128), lambda at: (0, 0)),
        ],
        out_shape=[
            jax.ShapeDtypeStruct((3, clients, width, half), jnp.bfloat16),
            jax.ShapeDtypeStruct((padded, 128), jnp.float32),
        ],
        scratch_shapes=[
            pltpu.VMEM((tokens, depth), jnp.bfloat16),
            pltpu.VMEM((3, clients, width, half), jnp.bfloat16),
            pltpu.VMEM((pair_count, 8, 128), jnp.float32),
        ],
        compiler_params=pltpu.CompilerParams(vmem_limit_bytes=60 * 2**20),
        cost_estimate=pl.CostEstimate(
            flops=2 * clients * tokens * (depth + 3 * width) * half,
            bytes_accessed=50 * 2**20,
            transcendentals=0,
        ),
        name="backward_all",
    )(every_residual, slope, active, hidden, block, down_half)


def sum_kernel(part_ref, total_ref, params_held, clients_held, summed, sends, receives):
    clients, params = clients_held.shape[0], params_held.shape[0]
    client, param = lax.axis_index("client"), lax.axis_index("param")
    barrier = pltpu.get_barrier_semaphore()
    for step in range(1, params):
        pl.semaphore_signal(
            barrier, inc=1, device_id=(client, lax.rem(param + step, params)),
            device_id_type=pl.DeviceIdType.MESH,
        )
    for step in range(1, clients):
        pl.semaphore_signal(
            barrier, inc=1, device_id=(lax.rem(client + step, clients), param),
            device_id_type=pl.DeviceIdType.MESH,
        )
    pl.semaphore_wait(barrier, params + clients - 2)

    def exchange(source, held, me, count, target, first):
        held[me] = source[...]
        copies = []
        for step in range(1, count):
            copy = pltpu.make_async_remote_copy(
                src_ref=source,
                dst_ref=held.at[me],
                send_sem=sends.at[first + step],
                recv_sem=receives.at[first + step],
                device_id=target(lax.rem(me + step, count)),
                device_id_type=pl.DeviceIdType.MESH,
            )
            copy.start()
            copies.append(copy)
        for copy in copies:
            copy.wait()
        total = held[0]
        for at in range(1, count):
            total = total + held[at]
        return total

    summed[...] = exchange(part_ref, params_held, param, params, lambda to: (client, to), 0)
    total_ref[...] = exchange(summed, clients_held, client, clients, lambda to: (to, param), params)


def sum_everywhere(part):
    clients, params = lax.axis_size("client"), lax.axis_size("param")
    return pl.pallas_call(
        sum_kernel,
        in_specs=[pl.BlockSpec(memory_space=pltpu.VMEM)],
        out_specs=pl.BlockSpec(memory_space=pltpu.VMEM),
        out_shape=jax.ShapeDtypeStruct(part.shape, part.dtype),
        scratch_shapes=[
            pltpu.VMEM((params,) + part.shape, part.dtype),
            pltpu.VMEM((clients,) + part.shape, part.dtype),
            pltpu.VMEM(part.shape, part.dtype),
            pltpu.SemaphoreType.DMA((params + clients,)),
            pltpu.SemaphoreType.DMA((params + clients,)),
        ],
        compiler_params=pltpu.CompilerParams(collective_id=0, has_side_effects=True),
        name="sum_everywhere",
    )(part)


def place_count(clients, i, j):
    return i * clients - i * (i - 1) // 2 + (j - i)


def on_device_shared(inputs, targets, norm_gain, gate_weight, up_weight, down_weight, neighbours):
    token_count = inputs.shape[1]
    clients = lax.axis_size("client")
    params = lax.axis_size("param")
    client = lax.axis_index("client")
    width = inputs.shape[2]
    depth = width * params
    core = client % PAIR
    half = gate_weight.shape[1] // PAIR
    chip_rows = depth // clients * PAIR
    factor = 1.0 / math.sqrt(token_count)

    own = lax.all_gather(inputs, "param", axis=2, tiled=True)[0]
    every_input = lax.all_gather(inputs[0], ("client", "param"), axis=0)
    normed_own = rms_normed(own, norm_gain)
    gate_value = jnp.dot(normed_own, gate_weight, preferred_element_type=jnp.float32)
    up_value = jnp.dot(normed_own, up_weight, preferred_element_type=jnp.float32)
    hidden = (gelu_tanh(gate_value) * up_value).astype(jnp.bfloat16)
    partial_out = jnp.dot(hidden, down_weight, preferred_element_type=jnp.float32)
    out_share = lax.psum_scatter(
        partial_out.astype(jnp.bfloat16), "param", scatter_dimension=1, tiled=True
    ).astype(jnp.float32)
    local_residual = ((out_share - targets[0].astype(jnp.float32)) * factor).astype(jnp.bfloat16)
    every_residual = lax.all_gather(local_residual, ("client", "param"), axis=0)

    gate_half = lax.dynamic_slice_in_dim(gate_weight, core * half, half, 1)
    up_half = lax.dynamic_slice_in_dim(up_weight, core * half, half, 1)
    down_half = lax.dynamic_slice_in_dim(down_weight, core * half, half, 0)
    shape = (clients, params, token_count, width)
    slope, active, hidden, block = forward_all(
        every_input.reshape(shape), norm_gain, gate_half, up_half
    )
    deltas, partial_gram = backward_all(
        every_residual.reshape(shape), slope, active, hidden, block, down_half
    )
    upper = jnp.sum(sum_everywhere(partial_gram), axis=1)
    order = [
        [place_count(clients, min(i, j), max(i, j)) for j in range(clients)] for i in range(clients)
    ]
    gram = upper[jnp.asarray(order)]
    weights = krum_weights(gram, neighbours)
    updates = jnp.sum(weights[None, :, None, None] * deltas.astype(jnp.float32), axis=1)
    updates = updates.reshape(3, PAIR, chip_rows // PAIR, half)
    kept = lax.dynamic_index_in_dim(updates, core, 1, keepdims=False)
    sent = lax.dynamic_index_in_dim(updates, 1 - core, 1, keepdims=False)
    arrived = lax.ppermute(sent, "client", [(i, i ^ 1) for i in range(clients)])
    first = jnp.where(core == 0, kept, arrived)
    second = jnp.where(core == 0, arrived, kept)
    whole = jnp.concatenate([first, second], axis=2)
    return (whole[0], whole[1], whole[2], clients * weights)


def solution(mesh):
    in_specs = (
        P("client", None, "param"),
        P("client", None, "param"),
        P(),
        P(None, "param"),
        P(None, "param"),
        P("param", None),
        P(),
    )
    out_specs = (P("client", "param"), P("client", "param"), P("client", "param"), P())
    shared = mesh.shape["client"] <= 8 and mesh.shape["client"] == PAIR * mesh.shape["param"]
    body = on_device_shared if shared else on_device
    return jax.shard_map(
        body, mesh=mesh, in_specs=in_specs, out_specs=out_specs, check_vma=False
    )
```

```python
import functools
import math

import jax
import jax.numpy as jnp
from jax import lax
from jax.experimental import pallas as pl
from jax.experimental.pallas import tpu as pltpu
from jax.sharding import PartitionSpec as P


def gelu_tanh(values):
    return jax.nn.gelu(values, approximate=True)


def rms_normed(gathered, norm_gain):
    widened = gathered.astype(jnp.float32)
    inverse_rms = lax.rsqrt(jnp.mean(widened * widened, axis=-1, keepdims=True) + 1e-06)
    return (widened * inverse_rms * norm_gain).astype(jnp.bfloat16)


def krum_weights(gram, neighbours):
    client_count = gram.shape[0]
    diagonal = jnp.diagonal(gram)
    distance = diagonal[:, None] + diagonal[None, :] - 2.0 * gram
    row_index = lax.broadcasted_iota(jnp.int32, (client_count, client_count), 0)
    col_index = lax.broadcasted_iota(jnp.int32, (client_count, client_count), 1)
    distance = jnp.where(row_index == col_index, jnp.asarray(1e30, gram.dtype), distance)
    ordered = jnp.sort(distance, axis=1)
    scores = jnp.sum(
        jnp.where(col_index < neighbours[:, None], ordered, jnp.zeros_like(ordered)), axis=1
    )
    scaled = scores / jnp.mean(scores)
    exponent = jnp.exp(-4.0 * scaled)
    return exponent / jnp.sum(exponent)


def token_contract(left, right):
    return lax.dot_general(
        left, right, (((0,), (0,)), ((), ())), preferred_element_type=jnp.float32
    )


def pair_products(exchanged):
    flattened = exchanged.reshape(exchanged.shape[0], -1)
    return lax.dot_general(
        flattened, flattened, (((1,), (1,)), ((), ())), preferred_element_type=jnp.float32
    )


def weighted_sum(weights, exchanged):
    return jnp.sum(weights[:, None, None] * exchanged.astype(jnp.float32), axis=0)


def on_device(inputs, targets, norm_gain, gate_weight, up_weight, down_weight, neighbours):
    token_count = inputs.shape[1]
    factor = 1.0 / math.sqrt(token_count)
    gathered = lax.all_gather(inputs, "param", axis=2, tiled=True)
    normed = rms_normed(gathered[0], norm_gain)
    gate_value = jnp.dot(normed, gate_weight, preferred_element_type=jnp.float32)
    up_value = jnp.dot(normed, up_weight, preferred_element_type=jnp.float32)
    activated, gelu_back = jax.vjp(gelu_tanh, gate_value)
    hidden = (activated * up_value).astype(jnp.bfloat16)
    partial_out = jnp.dot(hidden, down_weight, preferred_element_type=jnp.float32)
    out_share = lax.psum_scatter(
        partial_out.astype(jnp.bfloat16), "param", scatter_dimension=1, tiled=True
    ).astype(jnp.float32)
    local_residual = ((out_share - targets[0].astype(jnp.float32)) * factor).astype(jnp.bfloat16)
    residual = lax.all_gather(local_residual, "param", axis=1, tiled=True)
    down_delta = (-token_contract(residual, hidden)).astype(jnp.bfloat16)
    back_hidden = lax.dot_general(
        residual, down_weight, (((1,), (1,)), ((), ())), preferred_element_type=jnp.float32
    )
    back_gate = gelu_back(back_hidden * up_value)[0].astype(jnp.bfloat16)
    back_up = (back_hidden * activated).astype(jnp.bfloat16)
    gate_delta = (-token_contract(normed, back_gate)).astype(jnp.bfloat16)
    up_delta = (-token_contract(normed, back_up)).astype(jnp.bfloat16)
    owned_gate, owned_up, owned_down = (
        lax.all_to_all(gate_delta[None], "client", split_axis=1, concat_axis=0, tiled=True),
        lax.all_to_all(up_delta[None], "client", split_axis=1, concat_axis=0, tiled=True),
        lax.all_to_all(down_delta[None], "client", split_axis=1, concat_axis=0, tiled=True),
    )
    partial_gram = pair_products(owned_gate) + pair_products(owned_up) + pair_products(owned_down)
    gram = lax.psum(partial_gram, ("client", "param"))
    weights = krum_weights(gram, neighbours)
    client_count = lax.axis_size("client")
    update_gate = weighted_sum(weights, owned_gate)
    update_up = weighted_sum(weights, owned_up)
    update_down = weighted_sum(weights, owned_down)
    return (update_gate, update_up, update_down, client_count * weights)

PAIR = 2


def gelu_parts(values):
    scale = math.sqrt(2.0 / math.pi)
    squared = values * values
    bent = jnp.tanh(scale * values * (1.0 + 0.044715 * squared))
    lifted = 0.5 * (1.0 + bent)
    slope = 0.5 * values * (1.0 - bent * bent) * scale * (1.0 + 3.0 * 0.044715 * squared)
    return values * lifted, lifted + slope


def forward_kernel(
    rows_ref, gain_ref, gate_ref, up_ref, slope_ref, active_ref, hidden_ref, block_ref, normed
):
    params, width = rows_ref.shape[0], rows_ref.shape[2] // 2
    chip = lax.axis_index("client") // PAIR
    total = 0.0
    for at in range(params):
        wide = unpacked(rows_ref[at]).astype(jnp.float32)
        total += jnp.sum(wide * wide, axis=1, keepdims=True)
    inverse = lax.rsqrt(total * (1.0 / (params * width)) + 1e-06)
    for at in range(params):
        wide = unpacked(rows_ref[at]).astype(jnp.float32)
        normed[:, at * width : (at + 1) * width] = (wide * inverse * gain_ref[at]).astype(jnp.bfloat16)
    block_ref[...] = (unpacked(rows_ref[chip]).astype(jnp.float32) * inverse * gain_ref[chip]).astype(jnp.bfloat16)
    gate = jnp.dot(normed[...], gate_ref[...], preferred_element_type=jnp.float32)
    up = jnp.dot(normed[...], up_ref[...], preferred_element_type=jnp.float32)
    active, slope = gelu_parts(gate)
    slope_ref[...] = slope * up
    active_ref[...] = active
    hidden_ref[...] = (active * up).astype(jnp.bfloat16)


def forward_all(every_input, norm_gain, gate_half, up_half):
    clients, params, rows, lanes = every_input.shape
    tokens, width = 2 * rows, lanes // 2
    depth, half = gate_half.shape
    client_block = lambda shape: pl.BlockSpec((None,) + shape, lambda at: (at,) + (0,) * len(shape))
    whole = lambda shape: pl.BlockSpec(shape, lambda at: (0,) * len(shape))
    return pl.pallas_call(
        forward_kernel,
        grid=(clients,),
        in_specs=[
            client_block((params, rows, lanes)),
            whole((params, 1, width)),
            whole((depth, half)),
            whole((depth, half)),
        ],
        out_specs=[client_block((tokens, half))] * 3 + [client_block((tokens, width))],
        out_shape=[
            jax.ShapeDtypeStruct((clients, tokens, half), jnp.float32),
            jax.ShapeDtypeStruct((clients, tokens, half), jnp.float32),
            jax.ShapeDtypeStruct((clients, tokens, half), jnp.bfloat16),
            jax.ShapeDtypeStruct((clients, tokens, width), jnp.bfloat16),
        ],
        scratch_shapes=[pltpu.VMEM((tokens, depth), jnp.bfloat16)],
        compiler_params=pltpu.CompilerParams(vmem_limit_bytes=56 * 2**20),
        cost_estimate=pl.CostEstimate(
            flops=4 * clients * tokens * depth * half, bytes_accessed=40 * 2**20, transcendentals=0
        ),
        name="forward_all",
    )(every_input, norm_gain.reshape(params, 1, width), gate_half, up_half)


def backward_kernel(
    rows_ref, slope_ref, active_ref, hidden_ref, block_ref, down_ref, delta_ref, gram_ref,
    residual, held, totals,
):
    params, width = rows_ref.shape[0], rows_ref.shape[2] // 2
    _, clients, rows, columns = held.shape
    step_at = pl.program_id(0)
    chip = lax.axis_index("client") // PAIR
    for at in range(params):
        residual[:, at * width : (at + 1) * width] = unpacked(rows_ref[at])
    back = lax.dot_general(
        residual[...], down_ref[...], (((1,), (1,)), ((), ())), preferred_element_type=jnp.float32
    )
    back_gate = (back * slope_ref[...]).astype(jnp.bfloat16)
    back_up = (back * active_ref[...]).astype(jnp.bfloat16)
    for kind, (left, right) in enumerate(
        ((block_ref[...], back_gate), (block_ref[...], back_up), (unpacked(rows_ref[chip]), hidden_ref[...]))
    ):
        delta = (-token_contract(left, right)).astype(jnp.bfloat16)
        delta_ref[kind] = delta
        held[kind, step_at] = delta

    @pl.when(step_at == clients - 1)
    def _():
        totals[...] = jnp.zeros_like(totals)
        pairs = [(i, j) for i in range(clients) for j in range(i, clients)]
        starts = [(at, min(128, columns - at)) for at in range(0, columns, 128)]

        def add_up(kind, begin, wide, repeat):
            def step(index, sums):
                row = pl.multiple_of(index * 16, 16)
                for at in range(begin, begin + wide * repeat, wide):
                    tiles = [
                        held[kind, client, pl.ds(row, 16), at : at + wide].astype(jnp.float32)
                        for client in range(clients)
                    ]
                    found = []
                    for (i, j), total in zip(pairs, sums):
                        product = tiles[i] * tiles[j]
                        found.append(total + (product[:8] + product[8:]))
                    sums = tuple(found)
                return sums

            zeros = tuple(jnp.zeros((8, wide), jnp.float32) for _ in pairs)
            sums = lax.fori_loop(0, rows // 16, step, zeros)
            for at, total in enumerate(sums):
                totals[at, :, :wide] += total

        lanes = columns // 128 * 128
        for kind in range(3):
            add_up(kind, 0, 128, lanes // 128)
            if columns - lanes:
                add_up(kind, lanes, columns - lanes, 1)
        gram_ref[...] = jnp.zeros_like(gram_ref)
        gram_ref[: len(pairs), :] = jnp.sum(totals[...], axis=1)


def backward_all(every_residual, slope, active, hidden, block, down_half):
    clients, params, packed_rows, lanes = every_residual.shape
    tokens, width = 2 * packed_rows, lanes // 2
    half, depth = down_half.shape
    pair_count = clients * (clients + 1) // 2
    padded = -(-pair_count // 8) * 8
    client_block = lambda shape: pl.BlockSpec((None,) + shape, lambda at: (at,) + (0,) * len(shape))
    return pl.pallas_call(
        backward_kernel,
        grid=(clients,),
        in_specs=[client_block((params, packed_rows, lanes))]
        + [client_block((tokens, half))] * 3
        + [client_block((tokens, width)), pl.BlockSpec((half, depth), lambda at: (0, 0))],
        out_specs=[
            pl.BlockSpec((3, None, width, half), lambda at: (0, at, 0, 0)),
            pl.BlockSpec((padded, 128), lambda at: (0, 0)),
        ],
        out_shape=[
            jax.ShapeDtypeStruct((3, clients, width, half), jnp.bfloat16),
            jax.ShapeDtypeStruct((padded, 128), jnp.float32),
        ],
        scratch_shapes=[
            pltpu.VMEM((tokens, depth), jnp.bfloat16),
            pltpu.VMEM((3, clients, width, half), jnp.bfloat16),
            pltpu.VMEM((pair_count, 8, 128), jnp.float32),
        ],
        compiler_params=pltpu.CompilerParams(vmem_limit_bytes=60 * 2**20),
        cost_estimate=pl.CostEstimate(
            flops=2 * clients * tokens * (depth + 3 * width) * half,
            bytes_accessed=50 * 2**20,
            transcendentals=0,
        ),
        name="backward_all",
    )(every_residual, slope, active, hidden, block, down_half)


COLUMN, ACROSS, ALONG, FIRST, SECOND, SHARED, DOWN = 0, 1, 2, 3, 4, 5, 10


def gather_kernel(block_ref, all_ref, local_sem, sends, receives):
    clients, params, rows, _ = all_ref.shape
    chips = clients // PAIR
    client, param = lax.axis_index("client"), lax.axis_index("param")
    chip, core = client // PAIR, lax.rem(client, PAIR)
    across = param + 1 - 2 * lax.rem(param, 2)
    along = param + 2 - 4 * (param // 2)
    far = params - 1 - param
    sibling = (client + 1 - 2 * core, param)
    to_across, to_along = (client, across), (client, along)
    above, below = (client + PAIR, param), (client - PAIR, param)

    barrier = pltpu.get_barrier_semaphore()

    def greet(target):
        pl.semaphore_signal(barrier, inc=1, device_id=target, device_id_type=pl.DeviceIdType.MESH)

    for target in (sibling, to_across, to_along):
        greet(target)
    pl.when(chip + 1 < chips)(lambda: greet(above))
    pl.when(chip > 0)(lambda: greet(below))
    beside = (chip + chips - 1) // chips + (2 * chips - 2 - chip) // chips
    pl.semaphore_wait(barrier, 3 + beside)

    def place(origin, owner, kind=COLUMN, of=core):
        whole = all_ref.at[origin * PAIR + of, owner]
        if kind == FIRST:
            return whole.at[pl.ds(0, rows // 2)]
        if kind == SECOND:
            return whole.at[pl.ds(rows // 2, rows // 2)]
        return whole

    def copy(source, landing, origin, send_kind, receive_kind, target):
        return pltpu.make_async_remote_copy(
            src_ref=source,
            dst_ref=landing,
            send_sem=sends.at[origin, send_kind],
            recv_sem=receives.at[origin, receive_kind],
            device_id=target,
            device_id_type=pl.DeviceIdType.MESH,
        )

    def arrived(origin, kind, landing):
        copy(landing, landing, origin, kind, kind, sibling).wait_recv()

    def share(origin, owner, kind, source=None):
        landing = place(origin, owner, kind)
        source = landing if source is None else source
        copy(source, landing, origin, SHARED + kind, SHARED + kind, sibling).start()

    def from_column(origin, steps, upward):
        landing = place(origin, param)
        source = block_ref
        if steps:
            arrived(origin, COLUMN, landing)
            source = landing
        if upward or not steps:
            pl.when(chip + 1 < chips)(
                lambda: copy(source, landing, origin, COLUMN, COLUMN, above).start()
            )
        if not upward or not steps:
            pl.when(chip > 0)(lambda: copy(source, landing, origin, DOWN, COLUMN, below).start())
        copy(source, landing, origin, ACROSS, ACROSS, to_across).start()
        copy(source, landing, origin, ALONG, ALONG, to_along).start()
        share(origin, param, COLUMN, source)

    def from_sides(origin):
        landing = place(origin, across)
        arrived(origin, ACROSS, landing)
        part = place(origin, across, FIRST)
        copy(part, part, origin, FIRST, FIRST, to_along).start()
        share(origin, across, ACROSS)
        landing = place(origin, along)
        arrived(origin, ALONG, landing)
        part = place(origin, along, SECOND)
        copy(part, part, origin, SECOND, SECOND, to_across).start()
        share(origin, along, ALONG)

    def from_corner(origin):
        for kind in (FIRST, SECOND):
            arrived(origin, kind, place(origin, far, kind))
            share(origin, far, kind)

    def finish(origin, steps, upward):
        owners = {COLUMN: param, ACROSS: across, ALONG: along, FIRST: far, SECOND: far}
        for kind, owner in owners.items():
            arrived(origin, SHARED + kind, place(origin, owner, kind, 1 - core))
            landing = place(origin, owner, kind)
            copy(landing, landing, origin, SHARED + kind, SHARED + kind, sibling).wait_send()
        whole, part = place(origin, param), place(origin, across, FIRST)

        def sent(source, kind):
            copy(source, source, origin, kind, kind, sibling).wait_send()

        sent(whole, ACROSS)
        sent(whole, ALONG)
        sent(part, FIRST)
        sent(part, SECOND)
        if upward or not steps:
            pl.when(chip + 1 < chips)(lambda: sent(whole, COLUMN))
        if not upward or not steps:
            pl.when(chip > 0)(lambda: sent(whole, DOWN))

    kept = pltpu.make_async_copy(block_ref, all_ref.at[client, param], local_sem)
    kept.start()

    def visit(steps, stage):
        if not 0 <= steps < chips:
            return
        if steps == 0:
            stage(chip, 0, True)
            return
        pl.when(chip >= steps)(lambda: stage(chip - steps, steps, True))
        pl.when(chip + steps < chips)(lambda: stage(chip + steps, steps, False))

    for steps in range(chips + 2):
        visit(steps, from_column)
        visit(steps - 1, lambda origin, at, upward: from_sides(origin))
        visit(steps - 2, lambda origin, at, upward: from_corner(origin))
    for steps in range(chips):
        visit(steps, finish)
    kept.wait()


def packed(block):
    rows = block.shape[0] // 2
    return jnp.concatenate([block[:rows], block[rows:]], axis=1)


def unpacked(block):
    width = block.shape[1] // 2
    return jnp.concatenate([block[:, :width], block[:, width:]], axis=0)


def gather_everything(block):
    clients, params = lax.axis_size("client"), lax.axis_size("param")
    return pl.pallas_call(
        gather_kernel,
        in_specs=[pl.BlockSpec(memory_space=pl.ANY)],
        out_specs=pl.BlockSpec(memory_space=pl.ANY),
        out_shape=jax.ShapeDtypeStruct((clients, params) + block.shape, block.dtype),
        scratch_shapes=[
            pltpu.SemaphoreType.DMA,
            pltpu.SemaphoreType.DMA((clients // PAIR, 11)),
            pltpu.SemaphoreType.DMA((clients // PAIR, 10)),
        ],
        compiler_params=pltpu.CompilerParams(collective_id=1, has_side_effects=True),
        name="gather_everything",
    )(block)


def sum_kernel(part_ref, total_ref, params_held, clients_held, summed, sends, receives):
    clients, params = clients_held.shape[0], params_held.shape[0]
    client, param = lax.axis_index("client"), lax.axis_index("param")
    barrier = pltpu.get_barrier_semaphore()
    for step in range(1, params):
        pl.semaphore_signal(
            barrier, inc=1, device_id=(client, lax.rem(param + step, params)),
            device_id_type=pl.DeviceIdType.MESH,
        )
    for step in range(1, clients):
        pl.semaphore_signal(
            barrier, inc=1, device_id=(lax.rem(client + step, clients), param),
            device_id_type=pl.DeviceIdType.MESH,
        )
    pl.semaphore_wait(barrier, params + clients - 2)

    def exchange(source, held, me, count, target, first):
        held[me] = source[...]
        copies = []
        for step in range(1, count):
            copy = pltpu.make_async_remote_copy(
                src_ref=source,
                dst_ref=held.at[me],
                send_sem=sends.at[first + step],
                recv_sem=receives.at[first + step],
                device_id=target(lax.rem(me + step, count)),
                device_id_type=pl.DeviceIdType.MESH,
            )
            copy.start()
            copies.append(copy)
        for copy in copies:
            copy.wait()
        total = held[0]
        for at in range(1, count):
            total = total + held[at]
        return total

    summed[...] = exchange(part_ref, params_held, param, params, lambda to: (client, to), 0)
    total_ref[...] = exchange(summed, clients_held, client, clients, lambda to: (to, param), params)


def sum_everywhere(part):
    clients, params = lax.axis_size("client"), lax.axis_size("param")
    return pl.pallas_call(
        sum_kernel,
        in_specs=[pl.BlockSpec(memory_space=pltpu.VMEM)],
        out_specs=pl.BlockSpec(memory_space=pltpu.VMEM),
        out_shape=jax.ShapeDtypeStruct(part.shape, part.dtype),
        scratch_shapes=[
            pltpu.VMEM((params,) + part.shape, part.dtype),
            pltpu.VMEM((clients,) + part.shape, part.dtype),
            pltpu.VMEM(part.shape, part.dtype),
            pltpu.SemaphoreType.DMA((params + clients,)),
            pltpu.SemaphoreType.DMA((params + clients,)),
        ],
        compiler_params=pltpu.CompilerParams(collective_id=0, has_side_effects=True),
        name="sum_everywhere",
    )(part)


def place_count(clients, i, j):
    return i * clients - i * (i - 1) // 2 + (j - i)


def on_device_shared(inputs, targets, norm_gain, gate_weight, up_weight, down_weight, neighbours):
    token_count = inputs.shape[1]
    clients = lax.axis_size("client")
    params = lax.axis_size("param")
    client = lax.axis_index("client")
    width = inputs.shape[2]
    depth = width * params
    core = client % PAIR
    half = gate_weight.shape[1] // PAIR
    chip_rows = depth // clients * PAIR
    factor = 1.0 / math.sqrt(token_count)

    every_input = gather_everything(packed(inputs[0]))
    own = lax.dynamic_index_in_dim(every_input, client, 0, keepdims=False)
    own = jnp.concatenate([unpacked(own[at]) for at in range(params)], axis=1)
    normed_own = rms_normed(own, norm_gain)
    gate_value = jnp.dot(normed_own, gate_weight, preferred_element_type=jnp.float32)
    up_value = jnp.dot(normed_own, up_weight, preferred_element_type=jnp.float32)
    hidden = (gelu_tanh(gate_value) * up_value).astype(jnp.bfloat16)
    partial_out = jnp.dot(hidden, down_weight, preferred_element_type=jnp.float32)
    out_share = lax.psum_scatter(
        partial_out.astype(jnp.bfloat16), "param", scatter_dimension=1, tiled=True
    ).astype(jnp.float32)
    local_residual = ((out_share - targets[0].astype(jnp.float32)) * factor).astype(jnp.bfloat16)
    every_residual = gather_everything(packed(local_residual))

    gate_half = lax.dynamic_slice_in_dim(gate_weight, core * half, half, 1)
    up_half = lax.dynamic_slice_in_dim(up_weight, core * half, half, 1)
    down_half = lax.dynamic_slice_in_dim(down_weight, core * half, half, 0)
    slope, active, hidden, block = forward_all(
        every_input, norm_gain, gate_half, up_half
    )
    deltas, partial_gram = backward_all(
        every_residual, slope, active, hidden, block, down_half
    )
    upper = jnp.sum(sum_everywhere(partial_gram), axis=1)
    order = [
        [place_count(clients, min(i, j), max(i, j)) for j in range(clients)] for i in range(clients)
    ]
    gram = upper[jnp.asarray(order)]
    weights = krum_weights(gram, neighbours)
    updates = jnp.sum(weights[None, :, None, None] * deltas.astype(jnp.float32), axis=1)
    updates = updates.reshape(3, PAIR, chip_rows // PAIR, half)
    kept = lax.dynamic_index_in_dim(updates, core, 1, keepdims=False)
    sent = lax.dynamic_index_in_dim(updates, 1 - core, 1, keepdims=False)
    arrived = lax.ppermute(sent, "client", [(i, i ^ 1) for i in range(clients)])
    first = jnp.where(core == 0, kept, arrived)
    second = jnp.where(core == 0, arrived, kept)
    whole = jnp.concatenate([first, second], axis=2)
    return (whole[0], whole[1], whole[2], clients * weights)


def solution(mesh):
    in_specs = (
        P("client", None, "param"),
        P("client", None, "param"),
        P(),
        P(None, "param"),
        P(None, "param"),
        P("param", None),
        P(),
    )
    out_specs = (P("client", "param"), P("client", "param"), P("client", "param"), P())
    shared = mesh.shape["client"] <= 8 and mesh.shape["client"] == PAIR * mesh.shape["param"]
    shared = shared and mesh.shape["param"] == 4
    body = on_device_shared if shared else on_device
    return jax.shard_map(
        body, mesh=mesh, in_specs=in_specs, out_specs=out_specs, check_vma=False
    )
```

```python
import functools
import math

import jax
import jax.numpy as jnp
from jax import lax
from jax.experimental import pallas as pl
from jax.experimental.pallas import tpu as pltpu
from jax.sharding import PartitionSpec as P


def gelu_tanh(values):
    return jax.nn.gelu(values, approximate=True)


def rms_normed(gathered, norm_gain):
    widened = gathered.astype(jnp.float32)
    inverse_rms = lax.rsqrt(jnp.mean(widened * widened, axis=-1, keepdims=True) + 1e-06)
    return (widened * inverse_rms * norm_gain).astype(jnp.bfloat16)


def krum_weights(gram, neighbours):
    client_count = gram.shape[0]
    diagonal = jnp.diagonal(gram)
    distance = diagonal[:, None] + diagonal[None, :] - 2.0 * gram
    row_index = lax.broadcasted_iota(jnp.int32, (client_count, client_count), 0)
    col_index = lax.broadcasted_iota(jnp.int32, (client_count, client_count), 1)
    distance = jnp.where(row_index == col_index, jnp.asarray(1e30, gram.dtype), distance)
    ordered = jnp.sort(distance, axis=1)
    scores = jnp.sum(
        jnp.where(col_index < neighbours[:, None], ordered, jnp.zeros_like(ordered)), axis=1
    )
    scaled = scores / jnp.mean(scores)
    exponent = jnp.exp(-4.0 * scaled)
    return exponent / jnp.sum(exponent)


def token_contract(left, right):
    return lax.dot_general(
        left, right, (((0,), (0,)), ((), ())), preferred_element_type=jnp.float32
    )


def pair_products(exchanged):
    flattened = exchanged.reshape(exchanged.shape[0], -1)
    return lax.dot_general(
        flattened, flattened, (((1,), (1,)), ((), ())), preferred_element_type=jnp.float32
    )


def weighted_sum(weights, exchanged):
    return jnp.sum(weights[:, None, None] * exchanged.astype(jnp.float32), axis=0)


def on_device(inputs, targets, norm_gain, gate_weight, up_weight, down_weight, neighbours):
    token_count = inputs.shape[1]
    factor = 1.0 / math.sqrt(token_count)
    gathered = lax.all_gather(inputs, "param", axis=2, tiled=True)
    normed = rms_normed(gathered[0], norm_gain)
    gate_value = jnp.dot(normed, gate_weight, preferred_element_type=jnp.float32)
    up_value = jnp.dot(normed, up_weight, preferred_element_type=jnp.float32)
    activated, gelu_back = jax.vjp(gelu_tanh, gate_value)
    hidden = (activated * up_value).astype(jnp.bfloat16)
    partial_out = jnp.dot(hidden, down_weight, preferred_element_type=jnp.float32)
    out_share = lax.psum_scatter(
        partial_out.astype(jnp.bfloat16), "param", scatter_dimension=1, tiled=True
    ).astype(jnp.float32)
    local_residual = ((out_share - targets[0].astype(jnp.float32)) * factor).astype(jnp.bfloat16)
    residual = lax.all_gather(local_residual, "param", axis=1, tiled=True)
    down_delta = (-token_contract(residual, hidden)).astype(jnp.bfloat16)
    back_hidden = lax.dot_general(
        residual, down_weight, (((1,), (1,)), ((), ())), preferred_element_type=jnp.float32
    )
    back_gate = gelu_back(back_hidden * up_value)[0].astype(jnp.bfloat16)
    back_up = (back_hidden * activated).astype(jnp.bfloat16)
    gate_delta = (-token_contract(normed, back_gate)).astype(jnp.bfloat16)
    up_delta = (-token_contract(normed, back_up)).astype(jnp.bfloat16)
    owned_gate, owned_up, owned_down = (
        lax.all_to_all(gate_delta[None], "client", split_axis=1, concat_axis=0, tiled=True),
        lax.all_to_all(up_delta[None], "client", split_axis=1, concat_axis=0, tiled=True),
        lax.all_to_all(down_delta[None], "client", split_axis=1, concat_axis=0, tiled=True),
    )
    partial_gram = pair_products(owned_gate) + pair_products(owned_up) + pair_products(owned_down)
    gram = lax.psum(partial_gram, ("client", "param"))
    weights = krum_weights(gram, neighbours)
    client_count = lax.axis_size("client")
    update_gate = weighted_sum(weights, owned_gate)
    update_up = weighted_sum(weights, owned_up)
    update_down = weighted_sum(weights, owned_down)
    return (update_gate, update_up, update_down, client_count * weights)

PAIR = 2


def gelu_parts(values):
    scale = math.sqrt(2.0 / math.pi)
    squared = values * values
    bent = jnp.tanh(scale * values * (1.0 + 0.044715 * squared))
    lifted = 0.5 * (1.0 + bent)
    slope = 0.5 * values * (1.0 - bent * bent) * scale * (1.0 + 3.0 * 0.044715 * squared)
    return values * lifted, lifted + slope


def forward_kernel(
    rows_ref, gain_ref, gate_ref, up_ref, slope_ref, active_ref, hidden_ref, block_ref, normed,
    gate_half, up_half,
):
    params, width = rows_ref.shape[0], rows_ref.shape[2] // 2
    chip = lax.axis_index("client") // PAIR
    half = gate_half.shape[1]
    for side in range(PAIR):

        @pl.when((pl.program_id(0) == 0) & (lax.rem(lax.axis_index("client"), PAIR) == side))
        def _(side=side):
            gate_half[...] = gate_ref[:, side * half : (side + 1) * half]
            up_half[...] = up_ref[:, side * half : (side + 1) * half]

    total = 0.0
    for at in range(params):
        wide = unpacked(rows_ref[at]).astype(jnp.float32)
        total += jnp.sum(wide * wide, axis=1, keepdims=True)
    inverse = lax.rsqrt(total * (1.0 / (params * width)) + 1e-06)
    for at in range(params):
        wide = unpacked(rows_ref[at]).astype(jnp.float32)
        normed[:, at * width : (at + 1) * width] = (wide * inverse * gain_ref[at]).astype(jnp.bfloat16)
    block_ref[...] = (unpacked(rows_ref[chip]).astype(jnp.float32) * inverse * gain_ref[chip]).astype(jnp.bfloat16)
    gate = jnp.dot(normed[...], gate_half[...], preferred_element_type=jnp.float32)
    up = jnp.dot(normed[...], up_half[...], preferred_element_type=jnp.float32)
    active, slope = gelu_parts(gate)
    slope_ref[...] = slope * up
    active_ref[...] = active
    hidden_ref[...] = (active * up).astype(jnp.bfloat16)


def forward_all(every_input, norm_gain, gate_weight, up_weight):
    clients, params, rows, lanes = every_input.shape
    tokens, width = 2 * rows, lanes // 2
    depth, half = gate_weight.shape[0], gate_weight.shape[1] // PAIR
    client_block = lambda shape: pl.BlockSpec((None,) + shape, lambda at: (at,) + (0,) * len(shape))
    whole = lambda shape: pl.BlockSpec(shape, lambda at: (0,) * len(shape))
    return pl.pallas_call(
        forward_kernel,
        grid=(clients,),
        in_specs=[
            client_block((params, rows, lanes)),
            whole((params, 1, width)),
            pl.BlockSpec(memory_space=pltpu.VMEM),
            pl.BlockSpec(memory_space=pltpu.VMEM),
        ],
        out_specs=[client_block((tokens, half))] * 3 + [client_block((tokens, width))],
        out_shape=[
            jax.ShapeDtypeStruct((clients, tokens, half), jnp.float32),
            jax.ShapeDtypeStruct((clients, tokens, half), jnp.float32),
            jax.ShapeDtypeStruct((clients, tokens, half), jnp.bfloat16),
            jax.ShapeDtypeStruct((clients, tokens, width), jnp.bfloat16),
        ],
        scratch_shapes=[
            pltpu.VMEM((tokens, depth), jnp.bfloat16),
            pltpu.VMEM((depth, half), jnp.bfloat16),
            pltpu.VMEM((depth, half), jnp.bfloat16),
        ],
        compiler_params=pltpu.CompilerParams(vmem_limit_bytes=56 * 2**20),
        cost_estimate=pl.CostEstimate(
            flops=4 * clients * tokens * depth * half, bytes_accessed=40 * 2**20, transcendentals=0
        ),
        name="forward_all",
    )(every_input, norm_gain.reshape(params, 1, width), gate_weight, up_weight)


def backward_kernel(
    rows_ref, slope_ref, active_ref, hidden_ref, block_ref, down_ref, delta_ref, gram_ref,
    residual, held, totals,
):
    params, width = rows_ref.shape[0], rows_ref.shape[2] // 2
    _, clients, rows, columns = held.shape
    step_at = pl.program_id(0)
    chip = lax.axis_index("client") // PAIR
    for at in range(params):
        residual[:, at * width : (at + 1) * width] = unpacked(rows_ref[at])
    first = pl.multiple_of(lax.rem(lax.axis_index("client"), PAIR) * columns, columns)
    back = lax.dot_general(
        residual[...], down_ref[pl.ds(first, columns), :], (((1,), (1,)), ((), ())), preferred_element_type=jnp.float32
    )
    back_gate = (back * slope_ref[...]).astype(jnp.bfloat16)
    back_up = (back * active_ref[...]).astype(jnp.bfloat16)
    for kind, (left, right) in enumerate(
        ((block_ref[...], back_gate), (block_ref[...], back_up), (unpacked(rows_ref[chip]), hidden_ref[...]))
    ):
        delta = (-token_contract(left, right)).astype(jnp.bfloat16)
        delta_ref[kind] = delta
        held[kind, step_at] = delta

    @pl.when(step_at == clients - 1)
    def _():
        totals[...] = jnp.zeros_like(totals)
        pairs = [(i, j) for i in range(clients) for j in range(i, clients)]
        starts = [(at, min(128, columns - at)) for at in range(0, columns, 128)]

        def add_up(kind, begin, wide, repeat):
            def step(index, sums):
                row = pl.multiple_of(index * 16, 16)
                for at in range(begin, begin + wide * repeat, wide):
                    tiles = [
                        held[kind, client, pl.ds(row, 16), at : at + wide].astype(jnp.float32)
                        for client in range(clients)
                    ]
                    found = []
                    for (i, j), total in zip(pairs, sums):
                        product = tiles[i] * tiles[j]
                        found.append(total + (product[:8] + product[8:]))
                    sums = tuple(found)
                return sums

            zeros = tuple(jnp.zeros((8, wide), jnp.float32) for _ in pairs)
            sums = lax.fori_loop(0, rows // 16, step, zeros)
            for at, total in enumerate(sums):
                totals[at, :, :wide] += total

        lanes = columns // 128 * 128
        for kind in range(3):
            add_up(kind, 0, 128, lanes // 128)
            if columns - lanes:
                add_up(kind, lanes, columns - lanes, 1)
        gram_ref[...] = jnp.zeros_like(gram_ref)
        gram_ref[: len(pairs), :] = jnp.sum(totals[...], axis=1)


def backward_all(every_residual, slope, active, hidden, block, down_weight):
    clients, params, packed_rows, lanes = every_residual.shape
    tokens, width = 2 * packed_rows, lanes // 2
    half, depth = down_weight.shape[0] // PAIR, down_weight.shape[1]
    pair_count = clients * (clients + 1) // 2
    padded = -(-pair_count // 8) * 8
    client_block = lambda shape: pl.BlockSpec((None,) + shape, lambda at: (at,) + (0,) * len(shape))
    return pl.pallas_call(
        backward_kernel,
        grid=(clients,),
        in_specs=[client_block((params, packed_rows, lanes))]
        + [client_block((tokens, half))] * 3
        + [client_block((tokens, width)), pl.BlockSpec(memory_space=pltpu.VMEM)],
        out_specs=[
            pl.BlockSpec((3, None, width, half), lambda at: (0, at, 0, 0)),
            pl.BlockSpec((padded, 128), lambda at: (0, 0)),
        ],
        out_shape=[
            jax.ShapeDtypeStruct((3, clients, width, half), jnp.bfloat16),
            jax.ShapeDtypeStruct((padded, 128), jnp.float32),
        ],
        scratch_shapes=[
            pltpu.VMEM((tokens, depth), jnp.bfloat16),
            pltpu.VMEM((3, clients, width, half), jnp.bfloat16),
            pltpu.VMEM((pair_count, 8, 128), jnp.float32),
        ],
        compiler_params=pltpu.CompilerParams(vmem_limit_bytes=60 * 2**20),
        cost_estimate=pl.CostEstimate(
            flops=2 * clients * tokens * (depth + 3 * width) * half,
            bytes_accessed=50 * 2**20,
            transcendentals=0,
        ),
        name="backward_all",
    )(every_residual, slope, active, hidden, block, down_weight)


COLUMN, ACROSS, ALONG, FIRST, SECOND, SHARED, DOWN = 0, 1, 2, 3, 4, 5, 10


def gather_kernel(block_ref, all_ref, local_sem, sends, receives):
    clients, params, rows, _ = all_ref.shape
    chips = clients // PAIR
    client, param = lax.axis_index("client"), lax.axis_index("param")
    chip, core = client // PAIR, lax.rem(client, PAIR)
    across = param + 1 - 2 * lax.rem(param, 2)
    along = param + 2 - 4 * (param // 2)
    far = params - 1 - param
    sibling = (client + 1 - 2 * core, param)
    to_across, to_along = (client, across), (client, along)
    above, below = (client + PAIR, param), (client - PAIR, param)

    barrier = pltpu.get_barrier_semaphore()

    def greet(target):
        pl.semaphore_signal(barrier, inc=1, device_id=target, device_id_type=pl.DeviceIdType.MESH)

    for target in (sibling, to_across, to_along):
        greet(target)
    pl.when(chip + 1 < chips)(lambda: greet(above))
    pl.when(chip > 0)(lambda: greet(below))
    beside = (chip + chips - 1) // chips + (2 * chips - 2 - chip) // chips
    pl.semaphore_wait(barrier, 3 + beside)

    def place(origin, owner, kind=COLUMN, of=core):
        whole = all_ref.at[origin * PAIR + of, owner]
        if kind == FIRST:
            return whole.at[pl.ds(0, rows // 2)]
        if kind == SECOND:
            return whole.at[pl.ds(rows // 2, rows // 2)]
        return whole

    def copy(source, landing, origin, send_kind, receive_kind, target):
        return pltpu.make_async_remote_copy(
            src_ref=source,
            dst_ref=landing,
            send_sem=sends.at[origin, send_kind],
            recv_sem=receives.at[origin, receive_kind],
            device_id=target,
            device_id_type=pl.DeviceIdType.MESH,
        )

    def arrived(origin, kind, landing):
        copy(landing, landing, origin, kind, kind, sibling).wait_recv()

    def share(origin, owner, kind, source=None):
        landing = place(origin, owner, kind)
        source = landing if source is None else source
        copy(source, landing, origin, SHARED + kind, SHARED + kind, sibling).start()

    def from_column(origin, steps, upward):
        landing = place(origin, param)
        source = block_ref
        if steps:
            arrived(origin, COLUMN, landing)
            source = landing
        if upward or not steps:
            pl.when(chip + 1 < chips)(
                lambda: copy(source, landing, origin, COLUMN, COLUMN, above).start()
            )
        if not upward or not steps:
            pl.when(chip > 0)(lambda: copy(source, landing, origin, DOWN, COLUMN, below).start())
        copy(source, landing, origin, ACROSS, ACROSS, to_across).start()
        copy(source, landing, origin, ALONG, ALONG, to_along).start()
        share(origin, param, COLUMN, source)

    def from_sides(origin):
        landing = place(origin, across)
        arrived(origin, ACROSS, landing)
        part = place(origin, across, FIRST)
        copy(part, part, origin, FIRST, FIRST, to_along).start()
        share(origin, across, ACROSS)
        landing = place(origin, along)
        arrived(origin, ALONG, landing)
        part = place(origin, along, SECOND)
        copy(part, part, origin, SECOND, SECOND, to_across).start()
        share(origin, along, ALONG)

    def from_corner(origin):
        for kind in (FIRST, SECOND):
            arrived(origin, kind, place(origin, far, kind))
            share(origin, far, kind)

    def finish(origin, steps, upward):
        owners = {COLUMN: param, ACROSS: across, ALONG: along, FIRST: far, SECOND: far}
        for kind, owner in owners.items():
            arrived(origin, SHARED + kind, place(origin, owner, kind, 1 - core))
            landing = place(origin, owner, kind)
            copy(landing, landing, origin, SHARED + kind, SHARED + kind, sibling).wait_send()
        whole, part = place(origin, param), place(origin, across, FIRST)

        def sent(source, kind):
            copy(source, source, origin, kind, kind, sibling).wait_send()

        sent(whole, ACROSS)
        sent(whole, ALONG)
        sent(part, FIRST)
        sent(part, SECOND)
        if upward or not steps:
            pl.when(chip + 1 < chips)(lambda: sent(whole, COLUMN))
        if not upward or not steps:
            pl.when(chip > 0)(lambda: sent(whole, DOWN))

    kept = pltpu.make_async_copy(block_ref, all_ref.at[client, param], local_sem)
    kept.start()

    def visit(steps, stage):
        if not 0 <= steps < chips:
            return
        if steps == 0:
            stage(chip, 0, True)
            return
        pl.when(chip >= steps)(lambda: stage(chip - steps, steps, True))
        pl.when(chip + steps < chips)(lambda: stage(chip + steps, steps, False))

    for steps in range(chips + 2):
        visit(steps, from_column)
        visit(steps - 1, lambda origin, at, upward: from_sides(origin))
        visit(steps - 2, lambda origin, at, upward: from_corner(origin))
    for steps in range(chips):
        visit(steps, finish)
    kept.wait()


def packed(block):
    rows = block.shape[0] // 2
    return jnp.concatenate([block[:rows], block[rows:]], axis=1)


def unpacked(block):
    width = block.shape[1] // 2
    return jnp.concatenate([block[:, :width], block[:, width:]], axis=0)


def gather_everything(block):
    clients, params = lax.axis_size("client"), lax.axis_size("param")
    return pl.pallas_call(
        gather_kernel,
        in_specs=[pl.BlockSpec(memory_space=pl.ANY)],
        out_specs=pl.BlockSpec(memory_space=pl.ANY),
        out_shape=jax.ShapeDtypeStruct((clients, params) + block.shape, block.dtype),
        scratch_shapes=[
            pltpu.SemaphoreType.DMA,
            pltpu.SemaphoreType.DMA((clients // PAIR, 11)),
            pltpu.SemaphoreType.DMA((clients // PAIR, 10)),
        ],
        compiler_params=pltpu.CompilerParams(collective_id=1, has_side_effects=True),
        name="gather_everything",
    )(block)


def weighted_kernel(weight_ref, delta_ref, kept_ref, sent_ref):
    clients, rows, _ = delta_ref.shape
    core = lax.rem(lax.axis_index("client"), PAIR)
    height = rows // PAIR
    for side, out_ref in ((core, kept_ref), (1 - core, sent_ref)):

        def step(index, carry, side=side, out_ref=out_ref):
            row = pl.multiple_of(index * 16, 16)
            from_row = pl.multiple_of(side * height + index * 16, 16)
            total = weight_ref[0] * delta_ref[0, pl.ds(from_row, 16), :].astype(jnp.float32)
            for client in range(1, clients):
                tile = delta_ref[client, pl.ds(from_row, 16), :].astype(jnp.float32)
                total = total + weight_ref[client] * tile
            out_ref[pl.ds(row, 16), :] = total
            return carry

        lax.fori_loop(0, height // 16, step, 0, unroll=2)


def weighted_halves(weights, deltas):
    kinds, clients, rows, half = deltas.shape
    shape = jax.ShapeDtypeStruct((kinds, rows // PAIR, half), jnp.float32)
    return pl.pallas_call(
        weighted_kernel,
        grid=(kinds,),
        in_specs=[
            pl.BlockSpec(memory_space=pltpu.SMEM),
            pl.BlockSpec((None, clients, rows, half), lambda kind: (kind, 0, 0, 0)),
        ],
        out_specs=[pl.BlockSpec((None, rows // PAIR, half), lambda kind: (kind, 0, 0))] * 2,
        out_shape=[shape, shape],
        compiler_params=pltpu.CompilerParams(vmem_limit_bytes=40 * 2**20),
        name="weighted_halves",
    )(weights, deltas)


def sum_kernel(part_ref, total_ref, params_held, clients_held, summed, sends, receives):
    clients, params = clients_held.shape[0], params_held.shape[0]
    client, param = lax.axis_index("client"), lax.axis_index("param")
    barrier = pltpu.get_barrier_semaphore()
    for step in range(1, params):
        pl.semaphore_signal(
            barrier, inc=1, device_id=(client, lax.rem(param + step, params)),
            device_id_type=pl.DeviceIdType.MESH,
        )
    for step in range(1, clients):
        pl.semaphore_signal(
            barrier, inc=1, device_id=(lax.rem(client + step, clients), param),
            device_id_type=pl.DeviceIdType.MESH,
        )
    pl.semaphore_wait(barrier, params + clients - 2)

    def exchange(source, held, me, count, target, first):
        held[me] = source[...]
        copies = []
        for step in range(1, count):
            copy = pltpu.make_async_remote_copy(
                src_ref=source,
                dst_ref=held.at[me],
                send_sem=sends.at[first + step],
                recv_sem=receives.at[first + step],
                device_id=target(lax.rem(me + step, count)),
                device_id_type=pl.DeviceIdType.MESH,
            )
            copy.start()
            copies.append(copy)
        for copy in copies:
            copy.wait()
        total = held[0]
        for at in range(1, count):
            total = total + held[at]
        return total

    summed[...] = exchange(part_ref, params_held, param, params, lambda to: (client, to), 0)
    total_ref[...] = exchange(summed, clients_held, client, clients, lambda to: (to, param), params)


def sum_everywhere(part):
    clients, params = lax.axis_size("client"), lax.axis_size("param")
    return pl.pallas_call(
        sum_kernel,
        in_specs=[pl.BlockSpec(memory_space=pltpu.VMEM)],
        out_specs=pl.BlockSpec(memory_space=pltpu.VMEM),
        out_shape=jax.ShapeDtypeStruct(part.shape, part.dtype),
        scratch_shapes=[
            pltpu.VMEM((params,) + part.shape, part.dtype),
            pltpu.VMEM((clients,) + part.shape, part.dtype),
            pltpu.VMEM(part.shape, part.dtype),
            pltpu.SemaphoreType.DMA((params + clients,)),
            pltpu.SemaphoreType.DMA((params + clients,)),
        ],
        compiler_params=pltpu.CompilerParams(collective_id=0, has_side_effects=True),
        name="sum_everywhere",
    )(part)


def place_count(clients, i, j):
    return i * clients - i * (i - 1) // 2 + (j - i)


def on_device_shared(inputs, targets, norm_gain, gate_weight, up_weight, down_weight, neighbours):
    token_count = inputs.shape[1]
    clients = lax.axis_size("client")
    params = lax.axis_size("param")
    client = lax.axis_index("client")
    width = inputs.shape[2]
    depth = width * params
    core = client % PAIR
    half = gate_weight.shape[1] // PAIR
    chip_rows = depth // clients * PAIR
    factor = 1.0 / math.sqrt(token_count)

    every_input = gather_everything(packed(inputs[0]))
    own = lax.dynamic_index_in_dim(every_input, client, 0, keepdims=False)
    own = jnp.concatenate([unpacked(own[at]) for at in range(params)], axis=1)
    normed_own = rms_normed(own, norm_gain)
    gate_value = jnp.dot(normed_own, gate_weight, preferred_element_type=jnp.float32)
    up_value = jnp.dot(normed_own, up_weight, preferred_element_type=jnp.float32)
    hidden = (gelu_tanh(gate_value) * up_value).astype(jnp.bfloat16)
    partial_out = jnp.dot(hidden, down_weight, preferred_element_type=jnp.float32)
    out_share = lax.psum_scatter(
        partial_out.astype(jnp.bfloat16), "param", scatter_dimension=1, tiled=True
    ).astype(jnp.float32)
    local_residual = ((out_share - targets[0].astype(jnp.float32)) * factor).astype(jnp.bfloat16)
    every_residual = gather_everything(packed(local_residual))

    slope, active, hidden, block = forward_all(
        every_input, norm_gain, gate_weight, up_weight
    )
    deltas, partial_gram = backward_all(
        every_residual, slope, active, hidden, block, down_weight
    )
    upper = jnp.sum(sum_everywhere(partial_gram), axis=1)
    order = [
        [place_count(clients, min(i, j), max(i, j)) for j in range(clients)] for i in range(clients)
    ]
    gram = upper[jnp.asarray(order)]
    weights = krum_weights(gram, neighbours)
    kept, sent = weighted_halves(weights, deltas)
    arrived = lax.ppermute(sent, "client", [(i, i ^ 1) for i in range(clients)])
    first = jnp.where(core == 0, kept, arrived)
    second = jnp.where(core == 0, arrived, kept)
    whole = jnp.concatenate([first, second], axis=2)
    return (whole[0], whole[1], whole[2], clients * weights)


def solution(mesh):
    in_specs = (
        P("client", None, "param"),
        P("client", None, "param"),
        P(),
        P(None, "param"),
        P(None, "param"),
        P("param", None),
        P(),
    )
    out_specs = (P("client", "param"), P("client", "param"), P("client", "param"), P())
    shared = mesh.shape["client"] <= 8 and mesh.shape["client"] == PAIR * mesh.shape["param"]
    shared = shared and mesh.shape["param"] == 4
    body = on_device_shared if shared else on_device
    return jax.shard_map(
        body, mesh=mesh, in_specs=in_specs, out_specs=out_specs, check_vma=False
    )
```
